512 devices in a mesh: sec: 16 (over z), row: 32 (over x, y, core).
Axes of the slice: x: 4, y: 4, z: 16, core: 2. Of those that a mesh axis runs over, the one named last changes fastest.
Arguments:
- right_sides: bfloat16 [3072, 128, 256], P(('sec', 'row')), may hold values from -6 to 6
- inverses: bfloat16 [3072, 128, 128], P(('sec', 'row')), may hold values from -0.25 to 1.25, as said below
- coupling: bfloat16 [3072, 5, 128, 128], P(('sec', 'row')), may hold values from -0.1875 to 0.1875
- supernode_blocks: bfloat16 [7680, 128, 128], P(('sec', 'row')), may hold values from -0.109375 to 0.109375
- pattern: int32 [3072, 5], P(('sec', 'row')), may hold values from 0 to 191, as said below
Outputs:
- solution: bfloat16 [3072, 128, 256], P(('sec', 'row'))
The draws below stay inside these ranges and needn't reach their ends.
Inputs may be any that keep to these rules, and one draw needn't show every extreme that they name: `pattern`: block row 192 s + 6 d + a lists 5 distinct positions, all within 6 d - 1 to 6 d + 6, one of them 6 d + a; the lists of section 0 are unused. `inverses`: each block is lower triangular with unit diagonal.
All inputs are finite; a program needn't handle non-finite values.
Results may differ from the reference program's by a relative error of at most 0.027.
Values may be sent and summed in bfloat16 or wider, within the bound.
No kernel may reach another device: no remote copies, remote signals or barrier semaphores. Data moves between devices by JAX's collectives and lax.ppermute only.
A program may use at most 64 MiB of HBM per device.

```python
import jax
import jax.numpy as jnp
from jax import lax

BLK = 128
NRHS = 256
BD = 6
NNZ = 5
SB = 192
NB = 3072
NPAIR = 7680
N_SEC = 16
N_ROW = 32


def draw_inverses(key, part):
    key = jax.random.fold_in(key, 11)
    noise = jnp.clip(jax.random.normal(key, (NB, BLK, BLK), jnp.float32), -5.0, 5.0) * 0.05
    rows_id = jnp.arange(BLK)[:, None]
    cols_id = jnp.arange(BLK)[None, :]
    lower = (cols_id < rows_id).astype(jnp.float32)
    ident = (cols_id == rows_id).astype(jnp.float32)
    return (noise * lower[None] + ident[None]).astype(jnp.bfloat16)


def draw_pattern(key, part):
    key = jax.random.fold_in(key, 23)
    blocks = jnp.arange(NB, dtype=jnp.int32)
    within = blocks % SB
    device_pos = within // BD
    inner_pos = within % BD
    slots = jnp.arange(BD + 2, dtype=jnp.int32)
    position = device_pos[:, None] * BD - 1 + slots[None, :]
    valid = (position >= 0) & (position < SB)
    forced = slots[None, :] == inner_pos[:, None] + 1
    forced = forced | (inner_pos[:, None] == 0) & (slots[None, :] == 0)
    forced = forced | (inner_pos[:, None] == BD - 1) & (slots[None, :] == BD + 1)
    forced = forced & valid
    scores = jax.random.randint(key, (NB, BD + 2), 0, 1000, jnp.int32) * 16 + slots[None, :]
    scores = jnp.where(forced, scores + 100000, scores)
    scores = jnp.where(valid, scores, scores - 200000)
    _, chosen = jax.lax.top_k(scores, NNZ)
    return jnp.take_along_axis(position, chosen, axis=1).astype(jnp.int32)


def block_levels(key, extent, split, low, high):
    def one(axis_at, shards_of):
        heights = jax.random.uniform(jax.random.fold_in(jax.random.fold_in(key, 6), axis_at), (shards_of,), jnp.float32, low / len(split), high / len(split))
        return jnp.repeat(jnp.exp(heights), extent[axis_at] // shards_of).reshape((-1,) + (1,) * (len(extent) - axis_at - 1))

    level = one(*split[0])
    for cut in split[1:]:
        level = level * one(*cut)
    return level


def gaussian(own_key, shape, spread, bound, shards=(), held_as=jnp.bfloat16):
    result = jax.random.normal(own_key, shape, jnp.float32) * spread
    if len(shards) > 0:
        result = block_levels(own_key, shape, shards, -0.22, 0.18) * result
    return jnp.clip(result, min=-bound, max=bound).astype(held_as)


def setup_inputs(seed: int = 0) -> dict:
    splits = jax.random.split(jax.random.key(seed), 6)
    return {
        "right_sides": gaussian(splits[0], (NB, BLK, NRHS), 1.0, 6.0, ((0, 512),)),
        "inverses": draw_inverses(jax.random.fold_in(splits[5], 71), 0),
        "coupling": gaussian(splits[2], (NB, NNZ, BLK, BLK), (8 * BLK * NNZ // 5) ** -0.5, 0.1875, ((0, 512),)),
        "supernode_blocks": gaussian(splits[3], (NPAIR, BLK, BLK), (4 * BLK * BD) ** -0.5, 0.109375, ((0, 512),)),
        "pattern": draw_pattern(jax.random.fold_in(splits[5], 71), 0),
    }


def reference(right_sides, inverses, coupling, supernode_blocks, pattern):
    per_dev = BD * (BD - 1) // 2
    rhs_sec = right_sides.reshape(N_SEC, SB, BLK, NRHS)
    inv_sec = inverses.reshape(N_SEC, N_ROW, BD, BLK, BLK)
    cpl_sec = coupling.reshape(N_SEC, SB, NNZ, BLK, BLK)
    sup_sec = supernode_blocks.reshape(N_SEC, N_ROW, per_dev, BLK, BLK)
    pat_sec = pattern.reshape(N_SEC, SB, NNZ)

    def section(previous, inputs):
        rhs_s, inv_s, cpl_s, sup_s, pat_s = inputs
        picked = previous[pat_s.astype(jnp.int32)]
        updates = jnp.einsum('tnij,tnjc->tic', cpl_s.astype(jnp.float32), picked.astype(jnp.float32))
        remain = (rhs_s.astype(jnp.float32) - updates).reshape(N_ROW, BD, BLK, NRHS)
        solved = []
        for a in range(BD):
            residue = remain[:, a]
            for b in range(a):
                q = a * (a - 1) // 2 + b
                residue = residue - jnp.einsum('rij,rjc->ric', sup_s[:, q].astype(jnp.float32), solved[b].astype(jnp.float32))
            rounded = lax.optimization_barrier(residue.astype(jnp.bfloat16))
            value = jnp.einsum('rij,rjc->ric', inv_s[:, a].astype(jnp.float32), rounded.astype(jnp.float32))
            solved.append(value.astype(jnp.bfloat16))
        current = jnp.stack(solved, axis=1).reshape(SB, BLK, NRHS)
        return current, current

    start_val = jnp.zeros((SB, BLK, NRHS), jnp.bfloat16)
    _, outputs = lax.scan(section, start_val, (rhs_sec, inv_sec, cpl_sec, sup_sec, pat_sec))
    return outputs.reshape(NB, BLK, NRHS)
```

```python
import functools

import jax
import jax.numpy as jnp
from jax import lax
from jax.experimental import pallas as pl
from jax.experimental.pallas import tpu as pltpu
from jax.sharding import PartitionSpec as P

BLK = 128
BD = 6
NNZ = 5
WIN = BD + 2
CHUNKS = (128, 128)
PERIOD = 6
NT = (((1,), (1,)), ((), ()))


def dot_nt(x, y):
    return lax.dot_general(x, y, NT, preferred_element_type=jnp.float32)


def load(pairs, sems):
    copies = [pltpu.make_async_copy(src, dst, sems.at[i]) for i, (src, dst) in enumerate(pairs)]
    for copy in copies:
        copy.start()
    for copy in copies:
        copy.wait()


def substitute(out, known, sup, inv, a):
    if a:
        q = a * (a - 1) // 2
        coefs = jnp.concatenate([sup[q + b] for b in range(a)], axis=1)
        known = known - dot_nt(out[:, : a * BLK], coefs)
    out[:, a * BLK : (a + 1) * BLK] = dot_nt(known.astype(jnp.bfloat16), inv[a]).astype(jnp.bfloat16)


def sides_kernel(rhs_hbm, inv_hbm, sup_hbm, gt, rhs, inv, sup, sems):
    load(((inv_hbm, inv), (rhs_hbm, rhs), (sup_hbm, sup)), sems)
    for a in range(BD):
        substitute(gt, rhs[a].T.astype(jnp.float32), sup, inv, a)


def matrix_kernel(pattern_hbm, inv_hbm, cpl_hbm, sup_hbm, ht, ct, pattern, inv, cpl, sup, sems):
    load(((pattern_hbm, pattern), (inv_hbm, inv), (sup_hbm, sup), (cpl_hbm, cpl)), sems)
    first = lax.axis_index("row") * BD - 1
    for a in range(BD):
        ct[...] = jnp.zeros_like(ct)

        @pl.when(lax.axis_index("sec") > 0)
        def _():
            for n in range(NNZ):
                at = jnp.clip(pattern[a, n] - first, 0, WIN - 1)
                ct[pl.ds(pl.multiple_of(at * BLK, BLK), BLK), :] = cpl[a, n].T

        substitute(ht, ct[...].astype(jnp.float32), sup, inv, a)


def settle_kernel(_, kept):
    pass


def step_kernel(tick, rows, last, matrix, *refs):
    if last:
        *arrived, ht, _, gt = refs
    else:
        *arrived, ht, _, own, cross, mate, gt = refs if matrix else (*refs[:1], *refs)
    odd = lax.rem(lax.axis_index("row"), 2) == 1

    def emit(value):
        own[...] = value
        first, final = value[:, :BLK], value[:, (BD - 1) * BLK :]
        cross[...] = jnp.where(odd, final, first)
        mate[...] = jnp.where(odd, first, final)

    @pl.when(lax.axis_index("sec") == tick)
    def _():
        if not arrived:
            emit(gt[rows, :])
        else:
            main, cross_in, mate_in = (ref[...] for ref in arrived)
            low = jnp.where(odd, mate_in, cross_in)
            high = jnp.where(odd, cross_in, mate_in)
            window = jnp.concatenate([low, main, high], axis=1)
            update = jnp.dot(window, ht[...], preferred_element_type=jnp.float32)
            value = (gt[rows, :].astype(jnp.float32) - update).astype(jnp.bfloat16)
            gt[rows, :] = value
            if not last:
                emit(value)


def finish_kernel(gt, out):
    for a in range(BD):
        out[a] = gt[:, a * BLK : (a + 1) * BLK].T


def local(right_sides, inverses, coupling, supernode_blocks, pattern):
    sections = lax.axis_size("sec")
    devices = lax.axis_size("row")
    nrhs = right_sides.shape[2]
    bf16 = jnp.bfloat16
    vmem = pl.BlockSpec(memory_space=pltpu.VMEM)
    params = pltpu.CompilerParams(vmem_limit_bytes=16 * 2**20)

    pattern, right_sides, inverses, coupling, supernode_blocks = (
        pltpu.with_memory_space_constraint(x, pltpu.HBM)
        for x in (pattern, right_sides, inverses, coupling, supernode_blocks)
    )

    def prepared(kernel, rows, operands, scratch, flops, name):
        return pl.pallas_call(
            kernel,
            out_shape=pltpu.VMEM((rows, BD * BLK), bf16),
            in_specs=[pl.BlockSpec(memory_space=pltpu.HBM)] * len(operands),
            out_specs=vmem,
            scratch_shapes=scratch
            + [(pltpu.SMEM if x is pattern else pltpu.VMEM)(x.shape, x.dtype) for x in operands]
            + [pltpu.SemaphoreType.DMA((len(operands),))],
            compiler_params=params,
            cost_estimate=pl.CostEstimate(flops=flops, bytes_accessed=2**21, transcendentals=0),
            name=name,
        )(*operands)

    gt = prepared(sides_kernel, nrhs, (right_sides, inverses, supernode_blocks), [], 2**28, "sides")
    ht = prepared(
        matrix_kernel,
        WIN * BLK,
        (pattern, inverses, coupling, supernode_blocks),
        [pltpu.VMEM((WIN * BLK, BLK), bf16)],
        1_900_000_000,
        "matrix",
    )

    def settled(arrived):
        return pl.pallas_call(
            settle_kernel,
            out_shape=pltpu.VMEM(arrived.shape, bf16),
            in_specs=[vmem],
            out_specs=vmem,
            input_output_aliases={0: 0},
            compiler_params=params,
            cost_estimate=pl.CostEstimate(flops=1, bytes_accessed=0, transcendentals=0),
            name="settle",
        )(arrived)

    def step(tick, start, wide, arrived, gt):
        matrix = bool(arrived) or start > 0
        operands = (*arrived, ht, gt) if matrix else (gt,)
        last = tick == sections - 1
        results = [] if last else [pltpu.VMEM((wide, columns), bf16) for columns in (BD * BLK, BLK, BLK)]
        results.append(pltpu.VMEM((nrhs, BD * BLK), bf16))
        return pl.pallas_call(
            functools.partial(step_kernel, tick, slice(start, start + wide), last, matrix),
            out_shape=results,
            in_specs=[vmem] * len(operands),
            out_specs=[vmem] * len(results),
            input_output_aliases={len(operands) - 1: len(results) - 1},
            compiler_params=params,
            cost_estimate=pl.CostEstimate(flops=1900000000, bytes_accessed=0, transcendentals=0),
            name="step",
        )(*operands)

    def route(tick, target):
        return [
            (s * devices + d, (s + 1) * devices + target(d))
            for s in range(sections - 1)
            for d in range(devices)
            if s % PERIOD == tick % PERIOD and 0 <= target(d) < devices
        ]

    starts = [sum(CHUNKS[:k]) for k in range(len(CHUNKS))]
    arrived = [()] * len(CHUNKS)
    for tick in range(sections):
        for k, (start, wide) in enumerate(zip(starts, CHUNKS)):
            *outgoing, gt = step(tick, start, wide, arrived[k], gt)
            if outgoing:
                own, cross, mate = outgoing
                arrived[k] = (
                    settled(lax.ppermute(own, ("sec", "row"), route(tick, lambda d: d))),
                    lax.ppermute(cross, ("sec", "row"), route(tick, lambda d: d + 1 if d % 2 else d - 1)),
                    lax.ppermute(mate, ("sec", "row"), route(tick, lambda d: d ^ 1)),
                )
    return pl.pallas_call(
        finish_kernel,
        out_shape=jax.ShapeDtypeStruct((BD, BLK, nrhs), bf16),
        in_specs=[vmem],
        out_specs=vmem,
        compiler_params=params,
        name="finish",
    )(gt)


def solution(mesh):
    return jax.shard_map(
        local,
        mesh=mesh,
        in_specs=(
            P(("sec", "row"), None, None),
            P(("sec", "row"), None, None),
            P(("sec", "row"), None, None, None),
            P(("sec", "row"), None, None),
            P(("sec", "row"), None),
        ),
        out_specs=P(("sec", "row"), None, None),
        check_vma=False,
    )
```

```python
import functools

import jax
import jax.numpy as jnp
from jax import lax
from jax.experimental import pallas as pl
from jax.experimental.pallas import tpu as pltpu
from jax.sharding import PartitionSpec as P

BLK = 128
BD = 6
NNZ = 5
WIN = BD + 2
CHUNKS = (128, 128)
PERIOD = 6
NT = (((1,), (1,)), ((), ()))


def dot_nt(x, y):
    return lax.dot_general(x, y, NT, preferred_element_type=jnp.float32)


def loads(pairs, sems):
    copies = [pltpu.make_async_copy(src, dst, sems.at[i]) for i, (src, dst) in enumerate(pairs)]
    for copy in copies:
        copy.start()
    return copies


def substitute(out, known, sup, inv, a):
    if a:
        q = a * (a - 1) // 2
        coefs = jnp.concatenate([sup[q + b] for b in range(a)], axis=1)
        known = known - dot_nt(out[:, : a * BLK], coefs)
    out[:, a * BLK : (a + 1) * BLK] = dot_nt(known.astype(jnp.bfloat16), inv[a]).astype(jnp.bfloat16)


def sides_kernel(rhs_hbm, inv_hbm, sup_hbm, gt, rhs, inv, sup, sems):
    *early, late = loads(((inv_hbm, inv), (rhs_hbm, rhs), (sup_hbm, sup)), sems)
    for copy in early:
        copy.wait()
    for a in range(BD):
        if a == 1:
            late.wait()
        substitute(gt, rhs[a].T.astype(jnp.float32), sup, inv, a)


def matrix_kernel(pattern_hbm, inv_hbm, cpl_hbm, sup_hbm, ht, ct, pattern, inv, cpl, sup, sems):
    rows = [(cpl_hbm.at[a], cpl.at[a]) for a in range(BD)]
    *early, late = loads(((pattern_hbm, pattern), (inv_hbm, inv), *rows, (sup_hbm, sup)), sems)
    for copy in early[:2]:
        copy.wait()
    first = lax.axis_index("row") * BD - 1
    for a in range(BD):
        early[2 + a].wait()
        if a == 1:
            late.wait()
        ct[...] = jnp.zeros_like(ct)

        @pl.when(lax.axis_index("sec") > 0)
        def _():
            for n in range(NNZ):
                at = jnp.clip(pattern[a, n] - first, 0, WIN - 1)
                ct[pl.ds(pl.multiple_of(at * BLK, BLK), BLK), :] = cpl[a, n].T

        substitute(ht, ct[...].astype(jnp.float32), sup, inv, a)


def settle_kernel(_, kept):
    pass


def step_kernel(tick, rows, last, matrix, *refs):
    out = None
    if last == "whole":
        *arrived, ht, _, out, gt = refs
    elif last:
        *arrived, ht, _, gt = refs
    else:
        *arrived, ht, _, own, cross, mate, gt = refs if matrix else (*refs[:1], *refs)
    odd = lax.rem(lax.axis_index("row"), 2) == 1

    def emit(value):
        own[...] = value
        first, final = value[:, :BLK], value[:, (BD - 1) * BLK :]
        cross[...] = jnp.where(odd, final, first)
        mate[...] = jnp.where(odd, first, final)

    @pl.when(lax.axis_index("sec") == tick)
    def _():
        if not arrived:
            emit(gt[rows, :])
        else:
            main, cross_in, mate_in = (ref[...] for ref in arrived)
            low = jnp.where(odd, mate_in, cross_in)
            high = jnp.where(odd, cross_in, mate_in)
            window = jnp.concatenate([low, main, high], axis=1)
            update = jnp.dot(window, ht[...], preferred_element_type=jnp.float32)
            value = (gt[rows, :].astype(jnp.float32) - update).astype(jnp.bfloat16)
            gt[rows, :] = value
            if not last:
                emit(value)

    if out is not None:
        for a in range(BD):
            out[a] = gt[:, a * BLK : (a + 1) * BLK].T


def local(right_sides, inverses, coupling, supernode_blocks, pattern):
    sections = lax.axis_size("sec")
    devices = lax.axis_size("row")
    nrhs = right_sides.shape[2]
    bf16 = jnp.bfloat16
    vmem = pl.BlockSpec(memory_space=pltpu.VMEM)
    params = pltpu.CompilerParams(vmem_limit_bytes=16 * 2**20)

    pattern, right_sides, inverses, coupling, supernode_blocks = (
        pltpu.with_memory_space_constraint(x, pltpu.HBM)
        for x in (pattern, right_sides, inverses, coupling, supernode_blocks)
    )

    def prepared(kernel, rows, operands, scratch, flops, name):
        return pl.pallas_call(
            kernel,
            out_shape=pltpu.VMEM((rows, BD * BLK), bf16),
            in_specs=[pl.BlockSpec(memory_space=pltpu.HBM)] * len(operands),
            out_specs=vmem,
            scratch_shapes=scratch
            + [(pltpu.SMEM if x is pattern else pltpu.VMEM)(x.shape, x.dtype) for x in operands]
            + [pltpu.SemaphoreType.DMA((BD + 3,))],
            compiler_params=params,
            cost_estimate=pl.CostEstimate(flops=flops, bytes_accessed=2**21, transcendentals=0),
            name=name,
        )(*operands)

    gt = prepared(sides_kernel, nrhs, (right_sides, inverses, supernode_blocks), [], 2**28, "sides")
    ht = prepared(
        matrix_kernel,
        WIN * BLK,
        (pattern, inverses, coupling, supernode_blocks),
        [pltpu.VMEM((WIN * BLK, BLK), bf16)],
        1_900_000_000,
        "matrix",
    )

    def settled(arrived):
        return pl.pallas_call(
            settle_kernel,
            out_shape=pltpu.VMEM(arrived.shape, bf16),
            in_specs=[vmem],
            out_specs=vmem,
            input_output_aliases={0: 0},
            compiler_params=params,
            cost_estimate=pl.CostEstimate(flops=1, bytes_accessed=0, transcendentals=0),
            name="settle",
        )(arrived)

    def step(tick, start, wide, arrived, gt):
        matrix = bool(arrived) or start > 0
        operands = (*arrived, ht, gt) if matrix else (gt,)
        last = "" if tick < sections - 1 else "whole" if start + wide == nrhs else "chunk"
        results = [jax.ShapeDtypeStruct((BD, BLK, nrhs), bf16)] * (last == "whole") if last else [pltpu.VMEM((wide, columns), bf16) for columns in (BD * BLK, BLK, BLK)]
        results.append(pltpu.VMEM((nrhs, BD * BLK), bf16))
        return pl.pallas_call(
            functools.partial(step_kernel, tick, slice(start, start + wide), last, matrix),
            out_shape=results,
            in_specs=[vmem] * len(operands),
            out_specs=[vmem] * len(results),
            input_output_aliases={len(operands) - 1: len(results) - 1},
            compiler_params=params,
            cost_estimate=pl.CostEstimate(flops=1900000000, bytes_accessed=0, transcendentals=0),
            name="step",
        )(*operands)

    def route(tick, target):
        return [
            (s * devices + d, (s + 1) * devices + target(d))
            for s in range(sections - 1)
            for d in range(devices)
            if s % PERIOD == tick % PERIOD and 0 <= target(d) < devices
        ]

    starts = [sum(CHUNKS[:k]) for k in range(len(CHUNKS))]
    arrived = [()] * len(CHUNKS)
    for tick in range(sections):
        for k, (start, wide) in enumerate(zip(starts, CHUNKS)):
            *outgoing, gt = step(tick, start, wide, arrived[k], gt)
            if tick < sections - 1:
                own, cross, mate = outgoing
                arrived[k] = (
                    settled(lax.ppermute(own, ("sec", "row"), route(tick, lambda d: d))),
                    lax.ppermute(cross, ("sec", "row"), route(tick, lambda d: d + 1 if d % 2 else d - 1)),
                    lax.ppermute(mate, ("sec", "row"), route(tick, lambda d: d ^ 1)),
                )
    return outgoing[0]


def solution(mesh):
    return jax.shard_map(
        local,
        mesh=mesh,
        in_specs=(
            P(("sec", "row"), None, None),
            P(("sec", "row"), None, None),
            P(("sec", "row"), None, None, None),
            P(("sec", "row"), None, None),
            P(("sec", "row"), None),
        ),
        out_specs=P(("sec", "row"), None, None),
        check_vma=False,
    )
```

```python
import functools

import jax
import jax.numpy as jnp
from jax import lax
from jax.experimental import pallas as pl
from jax.experimental.pallas import tpu as pltpu
from jax.sharding import PartitionSpec as P

BLK = 128
BD = 6
NNZ = 5
WIN = BD + 2
CHUNKS = (128, 128)
PERIOD = 6
NT = (((1,), (1,)), ((), ()))


def dot_nt(x, y):
    return lax.dot_general(x, y, NT, preferred_element_type=jnp.float32)


def loads(pairs, sems):
    copies = [pltpu.make_async_copy(src, dst, sems.at[i]) for i, (src, dst) in enumerate(pairs)]
    for copy in copies:
        copy.start()
    return copies


def substitute(out, known, sup, inv, a):
    if a:
        q = a * (a - 1) // 2
        coefs = jnp.concatenate([sup[q + b] for b in range(a)], axis=1)
        known = known - dot_nt(out[:, : a * BLK], coefs)
    out[:, a * BLK : (a + 1) * BLK] = dot_nt(known.astype(jnp.bfloat16), inv[a]).astype(jnp.bfloat16)


def sides_kernel(rhs_hbm, inv_hbm, sup_hbm, gt, rhs, inv, sup, sems):
    *early, late = loads(((inv_hbm, inv), (rhs_hbm, rhs), (sup_hbm, sup)), sems)
    for copy in early:
        copy.wait()
    for a in range(BD):
        if a == 1:
            late.wait()
        substitute(gt, rhs[a].T.astype(jnp.float32), sup, inv, a)


def matrix_kernel(pattern_hbm, inv_hbm, cpl_hbm, sup_hbm, ht, ct, pattern, inv, cpl, sup, sems):
    rows = [(cpl_hbm.at[a], cpl.at[a]) for a in range(BD)]
    *early, late = loads(((pattern_hbm, pattern), (inv_hbm, inv), *rows, (sup_hbm, sup)), sems)
    for copy in early[:2]:
        copy.wait()
    first = lax.axis_index("row") * BD - 1
    for a in range(BD):
        early[2 + a].wait()
        if a == 1:
            late.wait()
        ct[...] = jnp.zeros_like(ct)

        @pl.when(lax.axis_index("sec") > 0)
        def _():
            for n in range(NNZ):
                at = jnp.clip(pattern[a, n] - first, 0, WIN - 1)
                ct[pl.ds(pl.multiple_of(at * BLK, BLK), BLK), :] = cpl[a, n].T

        substitute(ht, ct[...].astype(jnp.float32), sup, inv, a)


def settle_kernel(_, kept):
    pass


def step_kernel(tick, rows, last, matrix, *refs):
    out = None
    if last == "whole":
        *arrived, ht, _, out, gt = refs
    elif last:
        *arrived, ht, _, gt = refs
    else:
        *arrived, ht, _, own, cross, mate, gt = refs if matrix else (*refs[:1], *refs)
    odd = lax.rem(lax.axis_index("row"), 2) == 1

    def emit(value):
        own[...] = value
        first, final = value[:, :BLK], value[:, (BD - 1) * BLK :]
        cross[...] = jnp.where(odd, final, first)
        mate[...] = jnp.where(odd, first, final)

    @pl.when(lax.axis_index("sec") == tick)
    def _():
        if not arrived:
            emit(gt[rows, :])
        else:
            main, cross_in, mate_in = (ref[...] for ref in arrived)
            low = jnp.where(odd, mate_in, cross_in)
            high = jnp.where(odd, cross_in, mate_in)
            window = jnp.concatenate([low, main, high], axis=1)
            update = jnp.dot(window, ht[...], preferred_element_type=jnp.float32)
            value = (gt[rows, :].astype(jnp.float32) - update).astype(jnp.bfloat16)
            gt[rows, :] = value
            if not last:
                emit(value)

    if out is not None:
        for a in range(BD):
            out[a] = gt[:, a * BLK : (a + 1) * BLK].T


def local(right_sides, inverses, coupling, supernode_blocks, pattern):
    sections = lax.axis_size("sec")
    devices = lax.axis_size("row")
    nrhs = right_sides.shape[2]
    bf16 = jnp.bfloat16
    vmem = pl.BlockSpec(memory_space=pltpu.VMEM)
    params = pltpu.CompilerParams(vmem_limit_bytes=16 * 2**20)

    pattern, right_sides, inverses, coupling, supernode_blocks = (
        pltpu.with_memory_space_constraint(x, pltpu.HBM)
        for x in (pattern, right_sides, inverses, coupling, supernode_blocks)
    )

    def prepared(kernel, rows, operands, scratch, flops, name):
        return pl.pallas_call(
            kernel,
            out_shape=pltpu.VMEM((rows, BD * BLK), bf16),
            in_specs=[pl.BlockSpec(memory_space=pltpu.HBM)] * len(operands),
            out_specs=vmem,
            scratch_shapes=scratch
            + [(pltpu.SMEM if x is pattern else pltpu.VMEM)(x.shape, x.dtype) for x in operands]
            + [pltpu.SemaphoreType.DMA((BD + 3,))],
            compiler_params=params,
            cost_estimate=pl.CostEstimate(flops=flops, bytes_accessed=2**21, transcendentals=0),
            name=name,
        )(*operands)

    gt = prepared(sides_kernel, nrhs, (right_sides, inverses, supernode_blocks), [], 2**28, "sides")
    ht = prepared(
        matrix_kernel,
        WIN * BLK,
        (pattern, inverses, coupling, supernode_blocks),
        [pltpu.VMEM((WIN * BLK, BLK), bf16)],
        1_900_000_000,
        "matrix",
    )

    def settled(arrived):
        return pl.pallas_call(
            settle_kernel,
            out_shape=pltpu.VMEM(arrived.shape, bf16),
            in_specs=[vmem],
            out_specs=vmem,
            input_output_aliases={0: 0},
            compiler_params=params,
            cost_estimate=pl.CostEstimate(flops=1, bytes_accessed=0, transcendentals=0),
            name="settle",
        )(arrived)

    def step(tick, start, wide, arrived, gt):
        matrix = bool(arrived) or start > 0
        operands = (*arrived, ht, gt) if matrix else (gt,)
        last = "" if tick < sections - 1 else "whole" if start + wide == nrhs else "chunk"
        results = [jax.ShapeDtypeStruct((BD, BLK, nrhs), bf16)] * (last == "whole") if last else [pltpu.VMEM((wide, columns), bf16) for columns in (BD * BLK, BLK, BLK)]
        results.append(pltpu.VMEM((nrhs, BD * BLK), bf16))
        return pl.pallas_call(
            functools.partial(step_kernel, tick, slice(start, start + wide), last, matrix),
            out_shape=results,
            in_specs=[vmem] * len(operands),
            out_specs=[vmem] * len(results),
            input_output_aliases={len(operands) - 1: len(results) - 1},
            compiler_params=params,
            cost_estimate=pl.CostEstimate(flops=1900000000 if tick else 1, bytes_accessed=0, transcendentals=0),
            name="step",
        )(*operands)

    def route(tick, target):
        return [
            (s * devices + d, (s + 1) * devices + target(d))
            for s in range(sections - 1)
            for d in range(devices)
            if s % PERIOD == tick % PERIOD and 0 <= target(d) < devices
        ]

    starts = [sum(CHUNKS[:k]) for k in range(len(CHUNKS))]
    arrived = [()] * len(CHUNKS)
    for tick in range(sections):
        for k, (start, wide) in enumerate(zip(starts, CHUNKS)):
            *outgoing, gt = step(tick, start, wide, arrived[k], gt)
            if tick < sections - 1:
                own, cross, mate = outgoing
                arrived[k] = (
                    settled(lax.ppermute(own, ("sec", "row"), route(tick, lambda d: d))),
                    lax.ppermute(cross, ("sec", "row"), route(tick, lambda d: d + 1 if d % 2 else d - 1)),
                    lax.ppermute(mate, ("sec", "row"), route(tick, lambda d: d ^ 1)),
                )
    return outgoing[0]


def solution(mesh):
    return jax.shard_map(
        local,
        mesh=mesh,
        in_specs=(
            P(("sec", "row"), None, None),
            P(("sec", "row"), None, None),
            P(("sec", "row"), None, None, None),
            P(("sec", "row"), None, None),
            P(("sec", "row"), None),
        ),
        out_specs=P(("sec", "row"), None, None),
        check_vma=False,
    )
```
